256 devices in a mesh: dp: 32 (over x, z_hi, core), ctx: 8 (over y, z_lo).
Axes of the slice: x: 4, y: 4, z: 8 (z_hi: 4, z_lo: 2; z = z_hi * 2 + z_lo), core: 2. Of those that a mesh axis runs over, the one named last changes fastest.
Arguments:
- query: bfloat16 [65536, 4096], P(('dp', 'ctx'))
- keys: bfloat16 [65536, 512], P(('dp', 'ctx'))
- values: bfloat16 [65536, 512], P(('dp', 'ctx')), may hold values from -6 to 6
- segments: int32 [65536], P(('dp', 'ctx')), may hold values from 0 to 3, as said below
Outputs:
- attended: bfloat16 [65536, 4096], P(('dp', 'ctx'))
The draws below stay inside these ranges and needn't reach their ends.
Inputs may be any that keep to these rules, and one draw needn't show every extreme that they name: `segments`: constant over aligned blocks of 128 tokens; within each window of 2048 tokens the numbers start at 0 and rise by one at each document start, so a window holds 1 to 4 documents; some window holds 4.
All inputs are finite; a program needn't handle non-finite values.
Results may differ from the reference program's by a relative error of at most 0.0039.
Values may be sent and summed in bfloat16 or wider, within the bound.
No kernel may reach another device: no remote copies, remote signals or barrier semaphores. Data moves between devices by JAX's collectives and lax.ppermute only.
A program may use at most 64 MiB of HBM per device.

```python
import jax
import jax.numpy as jnp
from jax import lax

QH = 32
KVH = 4
HD = 128
ALIGN = 128
DOCS = 4
TOK_DEV = 256
WIN = 2048
TOKENS = 65536
N_DP = 32
N_CTX = 8


def draw_query(key, part):
    key = jax.random.fold_in(key, 7)
    drawn = jax.random.normal(key, (TOKENS, QH * HD), jnp.float32)
    return drawn.astype(jnp.bfloat16)


def draw_keys(key, part):
    key = jax.random.fold_in(key, 9)
    drawn = jax.random.normal(key, (TOKENS, KVH * HD), jnp.float32)
    return drawn.astype(jnp.bfloat16)


def draw_segments(key, part):
    key = jax.random.fold_in(key, 5)
    blocks = WIN // ALIGN
    count_key, pick_key, order_key = jax.random.split(key, 3)
    counts = jax.random.randint(count_key, (N_DP,), 1, DOCS + 1)
    picked = jax.random.randint(pick_key, (), 0, N_DP)
    counts = jnp.where(jnp.arange(N_DP) == picked, DOCS, counts)
    orders = jax.vmap(lambda one_key: jax.random.permutation(one_key, blocks - 1))(jax.random.split(order_key, N_DP))
    cuts = (orders < (counts - 1)[:, None]).astype(jnp.int32)
    numbers = jnp.concatenate([jnp.zeros((N_DP, 1), jnp.int32), jnp.cumsum(cuts, axis=1).astype(jnp.int32)], axis=1)
    return jnp.repeat(numbers, ALIGN, axis=1).reshape(TOKENS).astype(jnp.int32)


def shard_levels(rng, extent, pieces, low, high):
    def one(axis_at, blocks):
        heights = jax.random.uniform(jax.random.fold_in(jax.random.fold_in(rng, 6), axis_at), (blocks,), jnp.float32, low / len(pieces), high / len(pieces))
        return jnp.repeat(jnp.exp(heights), extent[axis_at] // blocks).reshape((-1,) + (1,) * (len(extent) - axis_at - 1))

    level = one(*pieces[0])
    for cut in pieces[1:]:
        level = level * one(*cut)
    return level


def scatter_about(rng, shape, spread, most, cuts=(), held_as=jnp.bfloat16):
    values = jax.random.normal(rng, shape, jnp.float32) * spread
    if len(cuts) > 0:
        values = shard_levels(rng, shape, cuts, -0.22, 0.18) * values
    return jnp.clip(values, min=-most, max=most).astype(held_as)


def setup_inputs(seed: int = 0) -> dict:
    seeds = jax.random.split(jax.random.key(seed), 5)
    query = draw_query(jax.random.fold_in(seeds[4], 71), 0)
    keys = draw_keys(jax.random.fold_in(seeds[4], 71), 0)
    values = scatter_about(seeds[2], (TOKENS, KVH * HD), 1.0, 6.0, ((0, 256),))
    segments = draw_segments(jax.random.fold_in(seeds[4], 71), 0)
    return {"query": query, "keys": keys, "values": values, "segments": segments}


masked_score = -1e30


def one_window(inputs):
    window_q, window_k, window_v, window_seg = inputs
    per_group = QH // KVH
    results = []
    for block_index in range(N_CTX):
        low_row = block_index * TOK_DEV
        high_row = low_row + TOK_DEV
        heads_q = window_q[low_row:high_row].astype(jnp.float32).reshape(TOK_DEV, KVH, per_group, HD)
        heads_k = window_k[:high_row].astype(jnp.float32).reshape(high_row, KVH, HD)
        heads_v = window_v[:high_row].astype(jnp.float32).reshape(high_row, KVH, HD)
        scores = jnp.einsum("rgjd,lgd->gjrl", heads_q, heads_k) * (HD ** -0.5)
        query_pos = jnp.arange(low_row, high_row)
        key_pos = jnp.arange(high_row)
        allowed = (window_seg[low_row:high_row, None] == window_seg[None, :high_row]) & (key_pos[None, :] <= query_pos[:, None])
        scores = jnp.where(allowed, scores, masked_score)
        row_top = jnp.max(scores, axis=-1, keepdims=True)
        weights = jnp.where(allowed, jnp.exp(scores - row_top), 0.0)
        totals = jnp.sum(weights, axis=-1)
        rounded = lax.optimization_barrier(weights.astype(jnp.bfloat16)).astype(jnp.float32)
        mixed = jnp.einsum("gjrl,lgd->gjrd", rounded, heads_v) / totals[..., None]
        results.append(mixed.transpose(2, 0, 1, 3).reshape(TOK_DEV, QH * HD).astype(jnp.bfloat16))
    return jnp.concatenate(results, axis=0)


def reference(query, keys, values, segments):
    outputs = lax.map(one_window, (query.reshape(N_DP, WIN, QH * HD), keys.reshape(N_DP, WIN, KVH * HD), values.reshape(N_DP, WIN, KVH * HD), segments.reshape(N_DP, WIN)))
    return outputs.reshape(TOKENS, QH * HD)
```

```python
import functools
import math

import jax
import jax.numpy as jnp
from jax import lax
from jax.experimental import pallas as pl
from jax.experimental.pallas import tpu as pltpu
from jax.sharding import PartitionSpec as P

QH = 32
KVH = 4
HD = 128
TOK = 256
SUB = 128
TAG = 16
PER = QH // KVH
SCALE = math.log2(math.e) / math.sqrt(HD)
SHUT = -1e30
OPEN = 3e38
SAFE = 1e30


def caps_of(tag_q, tag_k, earlier):
    key_docs = tag_k[...].astype(jnp.float32)
    key_docs = jnp.where(earlier, key_docs, -1.0)
    row = jnp.concatenate([key_docs[0:1], key_docs[8:9]], axis=1)
    query_docs = tag_q[...].astype(jnp.float32)
    caps = []
    for half in range(2):
        own = query_docs[8 * half : 8 * half + 1]
        own = jnp.concatenate([own, own], axis=1)
        caps.append(jnp.broadcast_to(jnp.where(row == own, OPEN, SHUT), (SUB, TOK)))
    return jnp.concatenate(caps, axis=0)


def own_cap(tag):
    docs = tag[...].astype(jnp.float32)
    rows = lax.broadcasted_iota(jnp.int32, (TOK, TOK), 0)
    cols = lax.broadcasted_iota(jnp.int32, (TOK, TOK), 1)
    same = jnp.broadcast_to(jnp.where(docs[0:1] == docs[8:9], 1, 0), (SUB, SUB))
    ones = jnp.ones((SUB, SUB), jnp.int32)
    same = jnp.concatenate(
        [
            jnp.concatenate([ones, ones], axis=1),
            jnp.concatenate([same, ones], axis=1),
        ],
        axis=0,
    )
    return jnp.where((cols <= rows) & (same == 1), OPEN, SHUT)


def scores_of(rows, keys):
    return lax.dot_general(
        rows, keys, (((1,), (1,)), ((), ())), preferred_element_type=jnp.float32
    )


def attend_kernel(blocks, own, first, last, others, *refs):
    refs = iter(refs)
    flags, query, own_keys, own_values = (next(refs) for _ in range(4))
    keys = [next(refs) for _ in range(blocks)]
    values = [next(refs) for _ in range(blocks)]
    if not first:
        mixed_in, totals_in = next(refs), next(refs)
    if last:
        far_keys = [next(refs) for _ in range(others)]
        far_values = [next(refs) for _ in range(others)]
        out = next(refs)
        key_buf, value_buf, sem = next(refs), next(refs), next(refs)
    else:
        mixed_out, totals_out = next(refs), next(refs)
    tag = own_values.at[TOK : TOK + TAG]
    self_keys = own_keys[...].astype(jnp.float32)

    parts = []
    if own:
        parts.append((own_keys[...], own_values[:TOK], own_cap(tag)))
    for at in range(blocks):
        cap = caps_of(tag, values[at].at[TOK : TOK + TAG], flags[at] > 0)
        parts.append((keys[at][...], values[at][:TOK], cap))

    lane = lax.broadcasted_iota(jnp.int32, (TOK, HD), 1)
    totals = None if first else totals_in[0]
    worst = None
    for head in range(PER):
        span = slice(head * HD, (head + 1) * HD)
        rows = query[:, span]
        shift = SCALE * jnp.sum(rows.astype(jnp.float32) * self_keys, axis=1, keepdims=True)
        mixed = None
        mark = jnp.where(lane == head, 1.0, 0.0).astype(jnp.bfloat16)
        if last:
            mark = jnp.ones((TOK, HD), jnp.bfloat16)
        for block_keys, block_values, cap in parts:
            scores = scores_of(rows, block_keys)
            weights = jnp.exp2(jnp.minimum(scores * SCALE - shift, cap)).astype(jnp.bfloat16)
            added = jnp.dot(
                weights,
                jnp.concatenate([block_values, mark], axis=1),
                preferred_element_type=jnp.float32,
            )
            mixed = added if mixed is None else mixed + added
        sums = mixed[:, HD:]
        mixed = mixed[:, :HD]
        if not first:
            mixed = mixed + mixed_in[:, span]
        if last:
            sums = sums + jnp.broadcast_to(totals[:, head : head + 1], (TOK, HD))
            out[:, span] = (mixed / sums).astype(jnp.bfloat16)
            high = jnp.where(sums < SAFE, 0.0, 1.0)
            worst = high if worst is None else jnp.maximum(worst, high)
        else:
            mixed_out[:, span] = mixed
            totals = sums if totals is None else totals + sums
    if not last:
        totals_out[0] = totals
        return

    group = pl.program_id(0)

    @pl.when(jnp.max(worst) > 0.0)
    def _():
        cols = pl.ds(pl.multiple_of(group * HD, HD), HD)
        for at in range(others):
            for source, target in ((far_keys, key_buf), (far_values, value_buf)):
                copy = pltpu.make_async_copy(source[at].at[:, cols], target.at[at], sem)
                copy.start()
                copy.wait()
        local = [(own_keys, own_values, None)]
        local += [(keys[at], values[at], flags[at]) for at in range(blocks)]
        local += [
            (key_buf.at[at], value_buf.at[at], flags[blocks + at]) for at in range(others)
        ]

        def capped(rows, place):
            block_keys, block_values, flag = local[place]
            scores = scores_of(rows, block_keys[...]) * SCALE
            if flag is None:
                return jnp.minimum(scores, own_cap(tag))
            return jnp.minimum(scores, caps_of(tag, block_values.at[TOK : TOK + TAG], flag > 0))

        def one_head(head, carry):
            span = pl.ds(pl.multiple_of(head * HD, HD), HD)
            rows = query[:, span]
            top = None
            for place in range(len(local)):
                high = jnp.max(capped(rows, place), axis=1, keepdims=True)
                top = high if top is None else jnp.maximum(top, high)
            mixed = jnp.zeros((TOK, 2 * HD), jnp.float32)
            for place in range(len(local)):
                weights = jnp.exp2(capped(rows, place) - top).astype(jnp.bfloat16)
                block_values = local[place][1][:TOK]
                mixed = mixed + jnp.dot(
                    weights,
                    jnp.concatenate([block_values, jnp.ones_like(block_values)], axis=1),
                    preferred_element_type=jnp.float32,
                )
            out[:, span] = (mixed[:, :HD] / mixed[:, HD:]).astype(jnp.bfloat16)
            return carry

        lax.fori_loop(0, PER, one_head, 0)


def attend(name, flags, query, own_pair, pairs, state=None, own=False, far=None, base=0, groups=KVH):
    blocks = len(pairs)
    first, last = state is None, far is not None
    wide = pl.BlockSpec((TOK, PER * HD), lambda g: (0, g + base))
    key_spec = pl.BlockSpec((TOK, HD), lambda g: (0, g + base))
    value_spec = pl.BlockSpec((TOK + TAG, HD), lambda g: (0, g + base))
    mixed_spec = pl.BlockSpec((TOK, PER * HD), lambda g: (0, g))
    total_spec = pl.BlockSpec((1, TOK, HD), lambda g: (g, 0, 0))
    anywhere = pl.BlockSpec(memory_space=pl.ANY)
    args = [flags, query, *own_pair, *(k for k, _ in pairs), *(v for _, v in pairs)]
    in_specs = [pl.BlockSpec(memory_space=pltpu.SMEM), wide, key_spec, value_spec]
    in_specs += [key_spec] * blocks + [value_spec] * blocks
    if not first:
        args += list(state)
        in_specs += [mixed_spec, total_spec]
    scratch = []
    if last:
        args += [k for k, _ in far] + [v for _, v in far]
        in_specs += [anywhere] * (2 * len(far))
        out_shape = jax.ShapeDtypeStruct((TOK, QH * HD), jnp.bfloat16)
        out_specs = wide
        scratch = [
            pltpu.VMEM((len(far), TOK, HD), jnp.bfloat16),
            pltpu.VMEM((len(far), TOK + TAG, HD), jnp.bfloat16),
            pltpu.SemaphoreType.DMA,
        ]
    else:
        out_shape = (
            jax.ShapeDtypeStruct((TOK, groups * PER * HD), jnp.float32),
            jax.ShapeDtypeStruct((groups, TOK, HD), jnp.float32),
        )
        out_specs = (mixed_spec, total_spec)
    work = (blocks + (1 if own else 0)) * groups * PER * TOK * TOK
    return pl.pallas_call(
        functools.partial(attend_kernel, blocks, own, first, last, len(far) if last else 0),
        grid=(groups,),
        in_specs=in_specs,
        out_specs=out_specs,
        out_shape=out_shape,
        scratch_shapes=scratch,
        compiler_params=pltpu.CompilerParams(vmem_limit_bytes=32 * 2**20),
        cost_estimate=pl.CostEstimate(
            flops=work * HD * 4, bytes_accessed=6 * 2**20, transcendentals=work
        ),
        name=name,
    )(*args)


def move(value, step_y, step_z):
    pairs = []
    for source in range(8):
        y, z = source // 2, source % 2
        pairs.append((source, (y + step_y) % 4 * 2 + (z + step_z) % 2))
    return lax.ppermute(value, "ctx", pairs)


def local(query, keys, values, segments):
    place = lax.axis_index("ctx")
    y, z = place // 2, place % 2

    up = functools.partial(move, step_y=1, step_z=0)
    down = functools.partial(move, step_y=-1, step_z=0)
    over = functools.partial(move, step_y=0, step_z=1)

    docs = segments.astype(jnp.bfloat16)
    tag = jnp.concatenate(
        [jnp.broadcast_to(docs[at * SUB], (TAG // 2, KVH * HD)) for at in range(2)], axis=0
    )
    tagged = jnp.concatenate([values, tag], axis=0)

    k_up, k_down, k_over = up(keys), down(keys), over(keys)
    v_up, v_down, v_over = up(tagged), down(tagged), over(tagged)
    k_far, v_far = up(k_up), down(v_down)
    k_up_over, k_down_over = over(k_up), over(k_down)
    v_up_over, v_down_over = up(v_over), down(v_over)
    k_far_over, v_far_over = up(k_up_over), down(v_down_over)

    own = (keys, tagged)
    near = [(k_up, v_up), (k_down, v_down), (k_over, v_over)]
    mid = [(k_far, v_far), (k_up_over, v_up_over), (k_down_over, v_down_over)]
    end = [(k_far_over, v_far_over)]

    def flags_of(steps):
        return jnp.stack(
            [((y + dy) % 4 * 2 + (z + dz) % 2 < place).astype(jnp.int32) for dy, dz in steps]
        )

    near_steps = [(-1, 0), (1, 0), (0, 1)]
    mid_steps = [(2, 0), (-1, 1), (1, 1)]
    end_steps = [(2, 1)]
    state = attend("near", flags_of(near_steps), query, own, near, own=True)
    state = attend("mid", flags_of(mid_steps), query, own, mid, state)
    return attend(
        "end", flags_of(end_steps + near_steps + mid_steps), query, own, end, state, far=near + mid
    )


def solution(mesh):
    placed = (
        P(("dp", "ctx"), None),
        P(("dp", "ctx"), None),
        P(("dp", "ctx"), None),
        P(("dp", "ctx")),
    )
    return jax.shard_map(
        local, mesh=mesh, in_specs=placed, out_specs=P(("dp", "ctx"), None), check_vma=False
    )
```

```python
import functools
import math

import jax
import jax.numpy as jnp
from jax import lax
from jax.experimental import pallas as pl
from jax.experimental.pallas import tpu as pltpu
from jax.sharding import PartitionSpec as P

QH = 32
KVH = 4
HD = 128
TOK = 256
SUB = 128
TAG = 16
PER = QH // KVH
WIDE = KVH * HD
SCALE = math.log2(math.e) / math.sqrt(HD)
SHUT = -1e30
OPEN = 3e38
SAFE = 1e30
START_ROWS = 2 * TOK
VMEM = pl.BlockSpec(memory_space=pltpu.VMEM)
SMEM = pl.BlockSpec(memory_space=pltpu.SMEM)


def aligned(index, size):
    start = index * size
    return pl.ds(start if isinstance(index, int) else pl.multiple_of(start, size), size)


def docs_of(block):
    tag = block[1][TOK : TOK + TAG, :HD].astype(jnp.float32)
    return tag[0:1], tag[8:9]


def cap_of(own, block):
    row = jnp.concatenate(docs_of(block), axis=1)
    caps = []
    for docs in docs_of(own):
        same = row == jnp.concatenate([docs, docs], axis=1)
        caps.append(jnp.where(same, OPEN, SHUT))
    return caps


def own_cap(own):
    rows = lax.broadcasted_iota(jnp.int32, (SUB, TOK), 0)
    cols = lax.broadcasted_iota(jnp.int32, (SUB, TOK), 1)
    return [
        jnp.where(cols <= rows + half * SUB, jnp.broadcast_to(cap, (SUB, TOK)), SHUT)
        for half, cap in enumerate(cap_of(own, own))
    ]


def capped(scores, caps):
    if not caps:
        return scores
    halves = [
        jnp.minimum(scores[half * SUB : (half + 1) * SUB], cap) for half, cap in enumerate(caps)
    ]
    return jnp.concatenate(halves, axis=0)


def scores_of(rows, keys):
    return lax.dot_general(
        rows, keys, (((1,), (1,)), ((), ())), preferred_element_type=jnp.float32
    )


def weighted(weights, values):
    return jnp.dot(
        weights.astype(jnp.bfloat16),
        jnp.concatenate([values, jnp.ones_like(values)], axis=1),
        preferred_element_type=jnp.float32,
    )


def head_sums(query, self_keys, parts, head):
    rows = query[:, aligned(head, HD)]
    shift = SCALE * jnp.sum(rows.astype(jnp.float32) * self_keys, axis=1, keepdims=True)
    total = None
    for keys, values, caps in parts:
        scores = capped(scores_of(rows, keys) * SCALE - shift, caps())
        added = weighted(jnp.exp2(scores), values)
        total = added if total is None else total + added
    return total


def per_head(own, query, blocks, caps, use, unroll=True):
    def one_group(group, carry):
        cols = aligned(group, HD)
        self_keys = own[0][:, cols].astype(jnp.float32)
        parts = [
            (keys[:, cols], values[:TOK, cols], cap) for (keys, values), cap in zip(blocks, caps)
        ]
        for at in range(PER):
            head = group * PER + at
            use(head, head_sums(query, self_keys, parts, head))
        return carry

    if unroll:
        for group in range(KVH):
            one_group(group, 0)
    else:
        lax.fori_loop(0, KVH, one_group, 0)


def stored_caps(own, blocks, store):
    readers = []
    for at, block in enumerate(blocks):
        for half, cap in enumerate(cap_of(own, block)):
            store[at, aligned(half, 8)] = jnp.broadcast_to(cap, (8, TOK))
        readers.append(lambda at=at: [store[at, 8 * half : 8 * half + 1] for half in range(2)])
    return readers


def tag_kernel(segments, values, tagged):
    tagged[:TOK] = values[...]
    rows = lax.broadcasted_iota(jnp.int32, (TAG, WIDE), 0)
    docs = jnp.where(rows < TAG // 2, segments[0], segments[SUB])
    tagged[TOK:] = docs.astype(jnp.float32).astype(jnp.bfloat16)


def own_kernel(query, keys, values, state):
    own = (keys, values)

    def put(head, sums):
        state[:TOK, aligned(head, 2 * HD)] = sums

    caps = own_cap(own)
    per_head(own, query, [own], [lambda: caps], put)


def pair_of(block):
    return (block.at[:TOK], block.at[TOK:])


def paired(refs):
    return [(refs[at], refs[at + 1]) for at in range(0, len(refs), 2)]


def earlier(steps):
    place = lax.axis_index("ctx")
    y, z = place // 2, place % 2
    return [((y + dy) % 4 * 2 + (z + dz) % 2 < place).astype(jnp.int32) for dy, dz in steps]


def more_kernel(steps, whole, query, *refs):
    count = len(steps)
    own = (refs[0], refs[1])
    blocks = paired(refs[2 : 2 * count + 2]) if not whole else [pair_of(r) for r in refs[2 : count + 2]]
    state_in, state, store = refs[-3:]
    flags = earlier(steps)
    every = flags[0]
    for at in range(1, count):
        every = every * flags[at]

    def add(head, sums):
        span = aligned(head, 2 * HD)
        state[:TOK, span] = state_in[:TOK, span] + sums

    def add_again(head, sums):
        state[:TOK, aligned(head, 2 * HD)] += sums

    @pl.when(every > 0)
    def _():
        per_head(own, query, blocks, stored_caps(own, blocks, store), add)

    @pl.when(every == 0)
    def _():
        state[:TOK] = state_in[:TOK]
        for at in range(count):

            @pl.when(flags[at] > 0)
            def _():
                one = [blocks[at]]
                per_head(own, query, one, stored_caps(own, one, store), add_again, unroll=False)


def last_kernel(steps, pairs, query, *refs):
    own, *blocks = paired(refs[: 2 * pairs + 2])
    blocks += [pair_of(block) for block in refs[2 * pairs + 2 : -6]]
    state, out, merged, worst, store, sem = refs[-6:]
    flags = earlier(steps)
    pieces = [(at * PER * HD, PER * HD) for at in range(KVH - 1)]
    pieces += [((QH - PER + 2 * at) * HD, 2 * HD) for at in range(PER // 2)]

    def out_copy(at):
        span = pl.ds(*pieces[at])
        return pltpu.make_async_copy(merged.at[:, span], out.at[:, span], sem.at[at])

    def put(head, sums):
        merged[:, aligned(head, HD)] = (sums[:, :HD] / sums[:, HD:]).astype(jnp.bfloat16)

    highs = []

    def finish(head, sums):
        sums = sums + state[:TOK, aligned(head, 2 * HD)]
        put(head, sums)
        high = jnp.where(sums[:, HD:] < SAFE, 0.0, 1.0).reshape(TOK // 8, 8, HD)
        highs.append(jnp.max(high, axis=0))
        for at, (start, size) in enumerate(pieces):
            if start + size == (head + 1) * HD:
                out_copy(at).start()
        if head == QH - 1:
            worst[...] = functools.reduce(jnp.maximum, highs)
            highs.clear()

    @pl.when(flags[0] > 0)
    def _():
        per_head(own, query, blocks[:1], stored_caps(own, blocks[:1], store), finish)

    @pl.when(flags[0] == 0)
    def _():
        for head in range(QH):
            finish(head, 0.0)

    bad = jnp.max(worst[...]) > 0.0
    for at in range(len(pieces)):
        out_copy(at).wait()

    @pl.when(bad)
    def _():
        def one_head(head, carry):
            cols = aligned(head // PER, HD)
            rows = query[:, aligned(head, HD)]

            def allowed(block, at):
                scores = scores_of(rows, block[0][:, cols]) * SCALE
                if at is None:
                    return capped(scores, own_cap(own))
                return jnp.where(flags[at] > 0, capped(scores, cap_of(own, block)), SHUT)

            places = [(own, None)] + [(block, at) for at, block in enumerate(blocks)]
            top = None
            for block, at in places:
                high = jnp.max(allowed(block, at), axis=1, keepdims=True)
                top = high if top is None else jnp.maximum(top, high)
            total = jnp.zeros((TOK, 2 * HD), jnp.float32)
            for block, at in places:
                weights = jnp.exp2(allowed(block, at) - top)
                total = total + weighted(weights, block[1][:TOK, cols])
            put(head, total)
            return carry

        lax.fori_loop(0, QH, one_head, 0)
        for at in range(len(pieces)):
            out_copy(at).start()
        for at in range(len(pieces)):
            out_copy(at).wait()


def params():
    return pltpu.CompilerParams(vmem_limit_bytes=8 * 2**20)


def cost(units):
    work = int(units * QH * TOK * TOK)
    return pl.CostEstimate(flops=work * HD * 4, bytes_accessed=2**20, transcendentals=work)


STATE = jax.ShapeDtypeStruct((TOK, 2 * QH * HD), jnp.float32)
START = jax.ShapeDtypeStruct((START_ROWS, 2 * QH * HD), jnp.float32)


def tag(segments, values):
    return pl.pallas_call(
        tag_kernel,
        in_specs=[SMEM, VMEM],
        out_specs=VMEM,
        out_shape=jax.ShapeDtypeStruct((TOK + TAG, WIDE), jnp.bfloat16),
        name="tag",
    )(segments, values)


def attend_own(query, own):
    return pl.pallas_call(
        own_kernel,
        in_specs=[VMEM] * 3,
        out_specs=VMEM,
        out_shape=START,
        compiler_params=params(),
        cost_estimate=cost(1),
        name="own",
    )(query, *own)


def cap_store(count):
    return pltpu.VMEM((count, 16, TOK), jnp.float32)


def attend_more(name, steps, query, own, blocks, state):
    count = len(steps)
    return pl.pallas_call(
        functools.partial(more_kernel, steps, len(blocks) == count),
        in_specs=[VMEM] * (4 + len(blocks)),
        out_specs=VMEM,
        out_shape=STATE,
        scratch_shapes=[cap_store(count)],
        compiler_params=params(),
        cost_estimate=cost(count),
        name=name,
    )(query, *own, *blocks, state)


def attend_last(steps, query, own, pairs, blocks, state):
    return pl.pallas_call(
        functools.partial(last_kernel, steps, len(pairs) // 2),
        in_specs=[VMEM] * (4 + len(pairs) + len(blocks)),
        out_specs=pl.BlockSpec(memory_space=pl.ANY),
        out_shape=jax.ShapeDtypeStruct((TOK, QH * HD), jnp.bfloat16),
        scratch_shapes=[
            pltpu.VMEM((TOK, QH * HD), jnp.bfloat16),
            pltpu.VMEM((8, HD), jnp.float32),
            cap_store(1),
            pltpu.SemaphoreType.DMA((KVH - 1 + PER // 2,)),
        ],
        compiler_params=params(),
        cost_estimate=cost(1),
        name="last",
    )(query, *own, *pairs, *blocks, state)


def move(value, step_y, step_z):
    pairs = []
    for source in range(8):
        y, z = source // 2, source % 2
        pairs.append((source, (y + step_y) % 4 * 2 + (z + step_z) % 2))
    return lax.ppermute(value, "ctx", pairs)


def local(query, keys, values, segments):
    up = functools.partial(move, step_y=1, step_z=0)
    down = functools.partial(move, step_y=-1, step_z=0)
    over = functools.partial(move, step_y=0, step_z=1)

    k_down, k_over, k_up = down(keys), over(keys), up(keys)
    tagged = tag(segments, values)
    own = (keys, tagged)
    v_down, v_over, v_up = down(tagged), over(tagged), up(tagged)
    state = attend_own(query, own)
    v_down, v_over, state = lax.optimization_barrier((v_down, v_over, state))
    b_down = jnp.concatenate([k_down, v_down], axis=0)
    b_over = jnp.concatenate([k_over, v_over], axis=0)
    b_far, b_down_over, b_up_over = down(b_down), over(b_down), up(b_over)
    near = [k_up, v_up, k_down, v_down, k_over, v_over]
    near_steps = [(-1, 0), (1, 0), (0, 1)]
    state = attend_more("near", near_steps, query, own, near, state)
    b_far, b_down_over, state = lax.optimization_barrier((b_far, b_down_over, state))
    end = [over(b_far[:TOK]), down(b_down_over[TOK:])]
    end_steps = [(2, 1)]
    mid = [b_far, b_up_over, b_down_over]
    mid_steps = [(2, 0), (-1, 1), (1, 1)]
    state = attend_more("mid", mid_steps, query, own, mid, state)
    steps = end_steps + near_steps + mid_steps
    return attend_last(steps, query, own, end + near, mid, state)


def solution(mesh):
    placed = (
        P(("dp", "ctx"), None),
        P(("dp", "ctx"), None),
        P(("dp", "ctx"), None),
        P(("dp", "ctx")),
    )
    return jax.shard_map(
        local, mesh=mesh, in_specs=placed, out_specs=P(("dp", "ctx"), None), check_vma=False
    )
```

```python
import functools
import math

import jax
import jax.numpy as jnp
from jax import lax
from jax.experimental import pallas as pl
from jax.experimental.pallas import tpu as pltpu
from jax.sharding import PartitionSpec as P

QH = 32
KVH = 4
HD = 128
TOK = 256
SUB = 128
TAG = 16
PER = QH // KVH
WIDE = KVH * HD
SCALE = math.log2(math.e) / math.sqrt(HD)
SHUT = -1e30
OPEN = 3e38
SAFE = 1e30
START_ROWS = 2 * TOK
VMEM = pl.BlockSpec(memory_space=pltpu.VMEM)
SMEM = pl.BlockSpec(memory_space=pltpu.SMEM)


def aligned(index, size):
    start = index * size
    return pl.ds(start if isinstance(index, int) else pl.multiple_of(start, size), size)


def docs_of(block):
    tag = block[1][TOK : TOK + TAG, :HD].astype(jnp.float32)
    return tag[0:1], tag[8:9]


def cap_of(own, block):
    row = jnp.concatenate(docs_of(block), axis=1)
    caps = []
    for docs in docs_of(own):
        same = row == jnp.concatenate([docs, docs], axis=1)
        caps.append(jnp.where(same, OPEN, SHUT))
    return caps


def own_cap(own):
    rows = lax.broadcasted_iota(jnp.int32, (SUB, TOK), 0)
    cols = lax.broadcasted_iota(jnp.int32, (SUB, TOK), 1)
    return [
        jnp.where(cols <= rows + half * SUB, jnp.broadcast_to(cap, (SUB, TOK)), SHUT)
        for half, cap in enumerate(cap_of(own, own))
    ]


def capped(scores, caps):
    if not caps:
        return scores
    halves = [
        jnp.minimum(scores[half * SUB : (half + 1) * SUB], cap) for half, cap in enumerate(caps)
    ]
    return jnp.concatenate(halves, axis=0)


def scores_of(rows, keys):
    return lax.dot_general(
        rows, keys, (((1,), (1,)), ((), ())), preferred_element_type=jnp.float32
    )


def weighted(weights, values):
    return jnp.dot(
        weights.astype(jnp.bfloat16),
        jnp.concatenate([values, jnp.ones_like(values)], axis=1),
        preferred_element_type=jnp.float32,
    )


def head_sums(own, query, blocks, caps, head):
    cols = aligned(head // PER, HD)
    rows = query[:, aligned(head, HD)]
    near = rows.astype(jnp.float32) * own[0][:, cols].astype(jnp.float32)
    shift = SCALE * jnp.sum(near, axis=1, keepdims=True)
    total = None
    for (keys, values), cap in zip(blocks, caps):
        scores = capped(scores_of(rows, keys[:, cols]) * SCALE - shift, cap())
        added = weighted(jnp.exp2(scores), values[:TOK, cols])
        total = added if total is None else total + added
    return total


def per_head(own, query, blocks, caps, use, unroll=True):
    if unroll:
        for head in range(QH):
            use(head, head_sums(own, query, blocks, caps, head))
        return

    def one_group(group, carry):
        for at in range(PER):
            head = group * PER + at
            use(head, head_sums(own, query, blocks, caps, head))
        return carry

    lax.fori_loop(0, KVH, one_group, 0)


def stored_caps(own, blocks, store):
    readers = []
    for at, block in enumerate(blocks):
        for half, cap in enumerate(cap_of(own, block)):
            store[at, aligned(half, 8)] = jnp.broadcast_to(cap, (8, TOK))
        readers.append(lambda at=at: [store[at, 8 * half : 8 * half + 1] for half in range(2)])
    return readers


def pack_kernel(segments, keys, values, block, tagged):
    rows = lax.broadcasted_iota(jnp.int32, (TAG, WIDE), 0)
    docs = jnp.where(rows < TAG // 2, segments[0], segments[SUB])
    docs = docs.astype(jnp.float32).astype(jnp.bfloat16)
    block[:TOK] = keys[...]
    for target, start in ((block, TOK), (tagged, 0)):
        target[start : start + TOK] = values[...]
        target[start + TOK :] = docs


def own_kernel(query, block, state):
    own = pair_of(block)

    def put(head, sums):
        state[:TOK, aligned(head, 2 * HD)] = sums

    caps = own_cap(own)
    per_head(own, query, [own], [lambda: caps], put)


def pair_of(block):
    return (block.at[:TOK], block.at[TOK:])


def paired(refs, whole):
    refs = iter(refs)
    return [pair_of(next(refs)) if one else (next(refs), next(refs)) for one in whole]


def flat(blocks):
    arrays = [part for block in blocks for part in (block if isinstance(block, tuple) else [block])]
    return arrays, tuple(not isinstance(block, tuple) for block in blocks)


def earlier(steps):
    place = lax.axis_index("ctx")
    y, z = place // 2, place % 2
    return [((y + dy) % 4 * 2 + (z + dz) % 2 < place).astype(jnp.int32) for dy, dz in steps]


def more_kernel(steps, whole, query, *refs):
    count = len(steps)
    own, *blocks = paired(refs[:-3], whole)
    state_in, state, store = refs[-3:]
    flags = earlier(steps)
    every = flags[0]
    for at in range(1, count):
        every = every * flags[at]

    def add(head, sums):
        span = aligned(head, 2 * HD)
        state[:TOK, span] = state_in[:TOK, span] + sums

    def add_again(head, sums):
        state[:TOK, aligned(head, 2 * HD)] += sums

    @pl.when(every > 0)
    def _():
        per_head(own, query, blocks, stored_caps(own, blocks, store), add)

    @pl.when(every == 0)
    def _():
        state[:TOK] = state_in[:TOK]
        for at in range(count):

            @pl.when(flags[at] > 0)
            def _():
                one = [blocks[at]]
                per_head(own, query, one, stored_caps(own, one, store), add_again, unroll=False)


def last_kernel(steps, whole, query, *refs):
    own, *blocks = paired(refs[:-6], whole)
    state, out, merged, worst, store, sem = refs[-6:]
    flags = earlier(steps)
    pieces = [(at * PER * HD, PER * HD) for at in range(KVH - 1)]
    pieces += [((QH - PER + 2 * at) * HD, 2 * HD) for at in range(PER // 2)]

    def out_copy(at):
        span = pl.ds(*pieces[at])
        return pltpu.make_async_copy(merged.at[:, span], out.at[:, span], sem.at[at])

    def put(head, sums):
        merged[:, aligned(head, HD)] = (sums[:, :HD] / sums[:, HD:]).astype(jnp.bfloat16)

    highs = []

    def finish(head, sums):
        sums = sums + state[:TOK, aligned(head, 2 * HD)]
        put(head, sums)
        high = jnp.where(sums[:, HD:] < SAFE, 0.0, 1.0).reshape(TOK // 8, 8, HD)
        highs.append(jnp.max(high, axis=0))
        for at, (start, size) in enumerate(pieces):
            if start + size == (head + 1) * HD:
                out_copy(at).start()
        if head == QH - 1:
            worst[...] = functools.reduce(jnp.maximum, highs)
            highs.clear()

    @pl.when(flags[0] > 0)
    def _():
        per_head(own, query, blocks[:1], stored_caps(own, blocks[:1], store), finish)

    @pl.when(flags[0] == 0)
    def _():
        for head in range(QH):
            finish(head, 0.0)

    bad = jnp.max(worst[...]) > 0.0
    for at in range(len(pieces)):
        out_copy(at).wait()

    @pl.when(bad)
    def _():
        def one_head(head, carry):
            cols = aligned(head // PER, HD)
            rows = query[:, aligned(head, HD)]

            def allowed(block, at):
                scores = scores_of(rows, block[0][:, cols]) * SCALE
                if at is None:
                    return capped(scores, own_cap(own))
                return jnp.where(flags[at] > 0, capped(scores, cap_of(own, block)), SHUT)

            places = [(own, None)] + [(block, at) for at, block in enumerate(blocks)]
            top = None
            for block, at in places:
                high = jnp.max(allowed(block, at), axis=1, keepdims=True)
                top = high if top is None else jnp.maximum(top, high)
            total = jnp.zeros((TOK, 2 * HD), jnp.float32)
            for block, at in places:
                weights = jnp.exp2(allowed(block, at) - top)
                total = total + weighted(weights, block[1][:TOK, cols])
            put(head, total)
            return carry

        lax.fori_loop(0, QH, one_head, 0)
        for at in range(len(pieces)):
            out_copy(at).start()
        for at in range(len(pieces)):
            out_copy(at).wait()


def params():
    return pltpu.CompilerParams(vmem_limit_bytes=8 * 2**20)


def cost(units):
    work = int(units * QH * TOK * TOK)
    return pl.CostEstimate(flops=work * HD * 4, bytes_accessed=2**20, transcendentals=work)


STATE = jax.ShapeDtypeStruct((TOK, 2 * QH * HD), jnp.float32)
START = jax.ShapeDtypeStruct((START_ROWS, 2 * QH * HD), jnp.float32)


def pack(segments, keys, values):
    return pl.pallas_call(
        pack_kernel,
        in_specs=[SMEM, VMEM, VMEM],
        out_specs=(VMEM, VMEM),
        out_shape=(
            jax.ShapeDtypeStruct((2 * TOK + TAG, WIDE), jnp.bfloat16),
            jax.ShapeDtypeStruct((TOK + TAG, WIDE), jnp.bfloat16),
        ),
        name="pack",
    )(segments, keys, values)


def attend_own(query, own):
    return pl.pallas_call(
        own_kernel,
        in_specs=[VMEM] * 2,
        out_specs=VMEM,
        out_shape=START,
        compiler_params=params(),
        cost_estimate=cost(1),
        name="own",
    )(query, own)


def cap_store(count):
    return pltpu.VMEM((count, 16, TOK), jnp.float32)


def attend_more(name, steps, query, own, blocks, state):
    arrays, whole = flat([own] + blocks)
    return pl.pallas_call(
        functools.partial(more_kernel, steps, whole),
        in_specs=[VMEM] * (2 + len(arrays)),
        out_specs=VMEM,
        out_shape=STATE,
        scratch_shapes=[cap_store(len(steps))],
        compiler_params=params(),
        cost_estimate=cost(len(steps)),
        name=name,
    )(query, *arrays, state)


def attend_last(steps, query, own, blocks, state):
    arrays, whole = flat([own] + blocks)
    return pl.pallas_call(
        functools.partial(last_kernel, steps, whole),
        in_specs=[VMEM] * (2 + len(arrays)),
        out_specs=pl.BlockSpec(memory_space=pl.ANY),
        out_shape=jax.ShapeDtypeStruct((TOK, QH * HD), jnp.bfloat16),
        scratch_shapes=[
            pltpu.VMEM((TOK, QH * HD), jnp.bfloat16),
            pltpu.VMEM((8, HD), jnp.float32),
            cap_store(1),
            pltpu.SemaphoreType.DMA((KVH - 1 + PER // 2,)),
        ],
        compiler_params=params(),
        cost_estimate=cost(1),
        name="last",
    )(query, *arrays, state)


def move(value, step_y, step_z):
    pairs = []
    for source in range(8):
        y, z = source // 2, source % 2
        pairs.append((source, (y + step_y) % 4 * 2 + (z + step_z) % 2))
    return lax.ppermute(value, "ctx", pairs)


def local(query, keys, values, segments):
    up = functools.partial(move, step_y=1, step_z=0)
    down = functools.partial(move, step_y=-1, step_z=0)
    over = functools.partial(move, step_y=0, step_z=1)

    k_down, k_over = down(keys), over(keys)
    own, tagged = pack(segments, keys, values)
    v_down, v_over = down(tagged), over(tagged)
    b_up = up(own)
    state = attend_own(query, own)
    v_down, v_over, state = lax.optimization_barrier((v_down, v_over, state))
    b_down = jnp.concatenate([k_down, v_down], axis=0)
    b_over = jnp.concatenate([k_over, v_over], axis=0)
    b_far, b_down_over, b_up_over = down(b_down), over(b_down), up(b_over)
    near = [b_up, (k_down, v_down), (k_over, v_over)]
    near_steps = [(-1, 0), (1, 0), (0, 1)]
    state = attend_more("near", near_steps, query, own, near, state)
    b_far, b_down_over, state = lax.optimization_barrier((b_far, b_down_over, state))
    end = [(over(b_far[:TOK]), down(b_down_over[TOK:]))]
    end_steps = [(2, 1)]
    mid = [b_far, b_up_over, b_down_over]
    mid_steps = [(2, 0), (-1, 1), (1, 1)]
    state = attend_more("mid", mid_steps, query, own, mid, state)
    return attend_last(end_steps + near_steps + mid_steps, query, own, end + near + mid, state)


def solution(mesh):
    placed = (
        P(("dp", "ctx"), None),
        P(("dp", "ctx"), None),
        P(("dp", "ctx"), None),
        P(("dp", "ctx")),
    )
    return jax.shard_map(
        local, mesh=mesh, in_specs=placed, out_specs=P(("dp", "ctx"), None), check_vma=False
    )
```

```python
import functools
import math

import jax
import jax.numpy as jnp
from jax import lax
from jax.experimental import pallas as pl
from jax.experimental.pallas import tpu as pltpu
from jax.sharding import PartitionSpec as P

QH = 32
KVH = 4
HD = 128
TOK = 256
SUB = 128
TAG = 16
PER = QH // KVH
WIDE = KVH * HD
SCALE = math.log2(math.e) / math.sqrt(HD)
SHUT = -1e30
OPEN = 3e38
SAFE = 1e30
START_ROWS = 2 * TOK
PIECES = ((0, 16), (16, 28), (28, 32))
NEAR_CASES = (((0, 1, 2), 2), ((0, 1), 1), ((0, 2), 1), ((0,), 1), ((2,), 1))
MID_CASES = (((0, 1, 2), 4), ((0, 1), 1), ((1,), 1))
VMEM = pl.BlockSpec(memory_space=pltpu.VMEM)
SMEM = pl.BlockSpec(memory_space=pltpu.SMEM)


def aligned(index, size):
    start = index * size
    return pl.ds(start if isinstance(index, int) else pl.multiple_of(start, size), size)


def docs_of(block):
    tag = block[1][TOK : TOK + TAG, :HD].astype(jnp.float32)
    return tag[0:1], tag[8:9]


def cap_of(own, block):
    row = jnp.concatenate(docs_of(block), axis=1)
    caps = []
    for docs in docs_of(own):
        same = row == jnp.concatenate([docs, docs], axis=1)
        caps.append(jnp.where(same, OPEN, SHUT))
    return caps


def own_cap(own):
    rows = lax.broadcasted_iota(jnp.int32, (SUB, TOK), 0)
    cols = lax.broadcasted_iota(jnp.int32, (SUB, TOK), 1)
    return [
        jnp.where(cols <= rows + half * SUB, jnp.broadcast_to(cap, (SUB, TOK)), SHUT)
        for half, cap in enumerate(cap_of(own, own))
    ]


def capped(scores, caps):
    if not caps:
        return scores
    halves = [
        jnp.minimum(scores[half * SUB : (half + 1) * SUB], cap) for half, cap in enumerate(caps)
    ]
    return jnp.concatenate(halves, axis=0)


def scores_of(rows, keys):
    return lax.dot_general(
        rows, keys, (((1,), (1,)), ((), ())), preferred_element_type=jnp.float32
    )


def weighted(weights, values):
    return jnp.dot(
        weights.astype(jnp.bfloat16),
        jnp.concatenate([values, jnp.ones_like(values)], axis=1),
        preferred_element_type=jnp.float32,
    )


def head_sums(own, query, blocks, caps, head, group=None):
    cols = aligned(head // PER if group is None else group, HD)
    rows = query[:, aligned(head, HD)]
    near = rows.astype(jnp.float32) * own[0][:, cols].astype(jnp.float32)
    shift = SCALE * jnp.sum(near, axis=1, keepdims=True)
    total = None
    for (keys, values), cap in zip(blocks, caps):
        scores = capped(scores_of(rows, keys[:, cols]) * SCALE - shift, cap())
        added = weighted(jnp.exp2(scores), values[:TOK, cols])
        total = added if total is None else total + added
    return total


def per_head(own, query, blocks, caps, use, groups=KVH):
    if groups == KVH:
        for head in range(QH):
            use(head, head_sums(own, query, blocks, caps, head))
        return

    def some_groups(step, carry):
        for at in range(groups * PER):
            head = step * groups * PER + at
            group = step * groups + at // PER
            use(head, head_sums(own, query, blocks, caps, head, group))
        return carry

    lax.fori_loop(0, KVH // groups, some_groups, 0)


def stored_caps(own, blocks, store):
    readers = []
    for at, block in enumerate(blocks):
        for half, cap in enumerate(cap_of(own, block)):
            store[at, aligned(half, 8)] = jnp.broadcast_to(cap, (8, TOK))
        readers.append(lambda at=at: [store[at, 8 * half : 8 * half + 1] for half in range(2)])
    return readers


def pack_kernel(segments, keys, values, block, tagged):
    rows = lax.broadcasted_iota(jnp.int32, (TAG, WIDE), 0)
    docs = jnp.where(rows < TAG // 2, segments[0], segments[SUB])
    docs = docs.astype(jnp.float32).astype(jnp.bfloat16)
    block[:TOK] = keys[...]
    for target, start in ((block, TOK), (tagged, 0)):
        target[start : start + TOK] = values[...]
        target[start + TOK :] = docs


def own_kernel(query, block, state):
    own = pair_of(block)

    def put(head, sums):
        state[:TOK, aligned(head, 2 * HD)] = sums

    caps = own_cap(own)
    per_head(own, query, [own], [lambda: caps], put)


def pair_of(block):
    return (block.at[:TOK], block.at[TOK:])


def paired(refs, whole):
    refs = iter(refs)
    return [pair_of(next(refs)) if one else (next(refs), next(refs)) for one in whole]


def flat(blocks):
    arrays = [part for block in blocks for part in (block if isinstance(block, tuple) else [block])]
    return arrays, tuple(not isinstance(block, tuple) for block in blocks)


def earlier(steps):
    place = lax.axis_index("ctx")
    y, z = place // 2, place % 2
    return [((y + dy) % 4 * 2 + (z + dz) % 2 < place).astype(jnp.int32) for dy, dz in steps]


def more_kernel(steps, cases, whole, query, *refs):
    count = len(steps)
    own, *blocks = paired(refs[:-3], whole)
    state_in, state, store = refs[-3:]
    flags = earlier(steps)
    code = sum(flag << at for at, flag in enumerate(flags))

    def add(head, sums):
        span = aligned(head, 2 * HD)
        state[:TOK, span] = state_in[:TOK, span] + sums

    rest = jnp.int32(1)
    for chosen, groups in cases:
        fits = (code == sum(1 << at for at in chosen)).astype(jnp.int32)
        rest = rest - fits

        @pl.when(fits > 0)
        def _():
            some = [blocks[at] for at in chosen]
            per_head(own, query, some, stored_caps(own, some, store), add, groups)

    @pl.when(rest > 0)
    def _():
        state[:TOK] = state_in[:TOK]


def last_kernel(steps, whole, query, *refs):
    own, *blocks = paired(refs[:-6], whole)
    state, out, merged, worst, store, sem = refs[-6:]
    flags = earlier(steps)
    pieces = [(start * HD, (end - start) * HD) for start, end in PIECES]

    def out_copy(at):
        span = pl.ds(*pieces[at])
        return pltpu.make_async_copy(merged.at[:, span], out.at[:, span], sem.at[at])

    def put(head, sums):
        merged[:, aligned(head, HD)] = (sums[:, :HD] / sums[:, HD:]).astype(jnp.bfloat16)

    highs = []

    def finish(head, sums):
        sums = sums + state[:TOK, aligned(head, 2 * HD)]
        put(head, sums)
        high = jnp.where(sums[:, HD:] < SAFE, 0.0, 1.0).reshape(TOK // 8, 8, HD)
        highs.append(jnp.max(high, axis=0))
        for at, (start, size) in enumerate(pieces):
            if start + size == (head + 1) * HD:
                out_copy(at).start()
        if head == QH - 1:
            worst[...] = functools.reduce(jnp.maximum, highs)
            highs.clear()

    @pl.when(flags[0] > 0)
    def _():
        per_head(own, query, blocks[:1], stored_caps(own, blocks[:1], store), finish)

    @pl.when(flags[0] == 0)
    def _():
        for head in range(QH):
            finish(head, 0.0)

    bad = jnp.max(worst[...]) > 0.0
    for at in range(len(pieces)):
        out_copy(at).wait()

    @pl.when(bad)
    def _():
        def one_head(head, carry):
            cols = aligned(head // PER, HD)
            rows = query[:, aligned(head, HD)]

            def allowed(block, at):
                scores = scores_of(rows, block[0][:, cols]) * SCALE
                if at is None:
                    return capped(scores, own_cap(own))
                return jnp.where(flags[at] > 0, capped(scores, cap_of(own, block)), SHUT)

            places = [(own, None)] + [(block, at) for at, block in enumerate(blocks)]
            top = None
            for block, at in places:
                high = jnp.max(allowed(block, at), axis=1, keepdims=True)
                top = high if top is None else jnp.maximum(top, high)
            total = jnp.zeros((TOK, 2 * HD), jnp.float32)
            for block, at in places:
                weights = jnp.exp2(allowed(block, at) - top)
                total = total + weighted(weights, block[1][:TOK, cols])
            put(head, total)
            return carry

        lax.fori_loop(0, QH, one_head, 0)
        for at in range(len(pieces)):
            out_copy(at).start()
        for at in range(len(pieces)):
            out_copy(at).wait()


def params():
    return pltpu.CompilerParams(vmem_limit_bytes=8 * 2**20)


def cost(units):
    work = int(units * QH * TOK * TOK)
    return pl.CostEstimate(flops=work * HD * 4, bytes_accessed=2**20, transcendentals=work)


STATE = jax.ShapeDtypeStruct((TOK, 2 * QH * HD), jnp.float32)
START = jax.ShapeDtypeStruct((START_ROWS, 2 * QH * HD), jnp.float32)


def pack(segments, keys, values):
    return pl.pallas_call(
        pack_kernel,
        in_specs=[SMEM, VMEM, VMEM],
        out_specs=(VMEM, VMEM),
        out_shape=(
            jax.ShapeDtypeStruct((2 * TOK + TAG, WIDE), jnp.bfloat16),
            jax.ShapeDtypeStruct((TOK + TAG, WIDE), jnp.bfloat16),
        ),
        name="pack",
    )(segments, keys, values)


def attend_own(query, own):
    return pl.pallas_call(
        own_kernel,
        in_specs=[VMEM] * 2,
        out_specs=VMEM,
        out_shape=START,
        compiler_params=params(),
        cost_estimate=cost(1),
        name="own",
    )(query, own)


def cap_store(count):
    return pltpu.VMEM((count, 16, TOK), jnp.float32)


def attend_more(name, steps, cases, query, own, blocks, state):
    arrays, whole = flat([own] + blocks)
    return pl.pallas_call(
        functools.partial(more_kernel, steps, cases, whole),
        in_specs=[VMEM] * (2 + len(arrays)),
        out_specs=VMEM,
        out_shape=STATE,
        scratch_shapes=[cap_store(len(steps))],
        compiler_params=params(),
        cost_estimate=cost(len(steps)),
        name=name,
    )(query, *arrays, state)


def attend_last(steps, query, own, blocks, state):
    arrays, whole = flat([own] + blocks)
    return pl.pallas_call(
        functools.partial(last_kernel, steps, whole),
        in_specs=[VMEM] * (2 + len(arrays)),
        out_specs=pl.BlockSpec(memory_space=pl.ANY),
        out_shape=jax.ShapeDtypeStruct((TOK, QH * HD), jnp.bfloat16),
        scratch_shapes=[
            pltpu.VMEM((TOK, QH * HD), jnp.bfloat16),
            pltpu.VMEM((8, HD), jnp.float32),
            cap_store(1),
            pltpu.SemaphoreType.DMA((len(PIECES),)),
        ],
        compiler_params=params(),
        cost_estimate=cost(1),
        name="last",
    )(query, *arrays, state)


def move(value, step_y, step_z, rows=range(4)):
    pairs = []
    for y in rows:
        for z in range(2):
            pairs.append((y * 2 + z, (y + step_y) % 4 * 2 + (z + step_z) % 2))
    return lax.ppermute(value, "ctx", pairs)


def local(query, keys, values, segments):
    up = functools.partial(move, step_y=1, step_z=0)
    down = functools.partial(move, step_y=-1, step_z=0)
    over = functools.partial(move, step_y=0, step_z=1)

    k_down, k_over = down(keys), over(keys)
    own, tagged = pack(segments, keys, values)
    v_down, v_over = down(tagged), over(tagged)
    b_up = up(own)
    state = attend_own(query, own)
    v_down, v_over, state = lax.optimization_barrier((v_down, v_over, state))
    b_down = jnp.concatenate([k_down, v_down], axis=0)
    b_over = jnp.concatenate([k_over, v_over], axis=0)
    b_far, b_down_over, b_up_over = down(b_down), over(b_down), up(b_over, rows=range(3))
    near = [b_up, (k_down, v_down), (k_over, v_over)]
    near_steps = [(-1, 0), (1, 0), (0, 1)]
    state = attend_more("near", near_steps, NEAR_CASES, query, own, near, state)
    b_far, b_down_over, state = lax.optimization_barrier((b_far, b_down_over, state))
    end = [(over(b_far[:TOK]), down(b_down_over[TOK:]))]
    end_steps = [(2, 1)]
    mid = [b_far, b_up_over, b_down_over]
    mid_steps = [(2, 0), (-1, 1), (1, 1)]
    state = attend_more("mid", mid_steps, MID_CASES, query, own, mid, state)
    return attend_last(end_steps + near_steps + mid_steps, query, own, end + near + mid, state)


def solution(mesh):
    placed = (
        P(("dp", "ctx"), None),
        P(("dp", "ctx"), None),
        P(("dp", "ctx"), None),
        P(("dp", "ctx")),
    )
    return jax.shard_map(
        local, mesh=mesh, in_specs=placed, out_specs=P(("dp", "ctx"), None), check_vma=False
    )
```

```python
import functools
import math

import jax
import jax.numpy as jnp
from jax import lax
from jax.experimental import pallas as pl
from jax.experimental.pallas import tpu as pltpu
from jax.sharding import PartitionSpec as P

QH = 32
KVH = 4
HD = 128
TOK = 256
SUB = 128
TAG = 16
PER = QH // KVH
WIDE = KVH * HD
SCALE = math.log2(math.e) / math.sqrt(HD)
SHUT = -1e30
OPEN = 3e38
SAFE = 1e30
START_ROWS = 2 * TOK
PIECES = ((0, 16), (16, 28), (28, 32))
NEAR_CASES = (((0, 1, 2), 2), ((0, 1), 1), ((0, 2), 1), ((0,), 1), ((2,), 1))
MID_CASES = (((0, 1, 2), 4), ((0, 1), 2), ((1,), 1))
VMEM = pl.BlockSpec(memory_space=pltpu.VMEM)
SMEM = pl.BlockSpec(memory_space=pltpu.SMEM)


def aligned(index, size):
    start = index * size
    return pl.ds(start if isinstance(index, int) else pl.multiple_of(start, size), size)


def docs_of(block):
    tag = block[1][TOK : TOK + TAG, :HD].astype(jnp.float32)
    return tag[0:1], tag[8:9]


def cap_of(own, block):
    row = jnp.concatenate(docs_of(block), axis=1)
    caps = []
    for docs in docs_of(own):
        same = row == jnp.concatenate([docs, docs], axis=1)
        caps.append(jnp.where(same, OPEN, SHUT))
    return caps


def own_cap(own):
    rows = lax.broadcasted_iota(jnp.int32, (SUB, TOK), 0)
    cols = lax.broadcasted_iota(jnp.int32, (SUB, TOK), 1)
    return [
        jnp.where(cols <= rows + half * SUB, jnp.broadcast_to(cap, (SUB, TOK)), SHUT)
        for half, cap in enumerate(cap_of(own, own))
    ]


def capped(scores, caps):
    if not caps:
        return scores
    halves = [
        jnp.minimum(scores[half * SUB : (half + 1) * SUB], cap) for half, cap in enumerate(caps)
    ]
    return jnp.concatenate(halves, axis=0)


def scores_of(rows, keys):
    return lax.dot_general(
        rows, keys, (((1,), (1,)), ((), ())), preferred_element_type=jnp.float32
    )


def weighted(weights, values):
    return jnp.dot(
        weights.astype(jnp.bfloat16),
        jnp.concatenate([values, jnp.ones_like(values)], axis=1),
        preferred_element_type=jnp.float32,
    )


def head_sums(own, query, blocks, caps, head, group=None):
    cols = aligned(head // PER if group is None else group, HD)
    rows = query[:, aligned(head, HD)]
    near = rows.astype(jnp.float32) * own[0][:, cols].astype(jnp.float32)
    shift = SCALE * jnp.sum(near, axis=1, keepdims=True)
    total = None
    for (keys, values), cap in zip(blocks, caps):
        scores = capped(scores_of(rows, keys[:, cols]) * SCALE - shift, cap())
        added = weighted(jnp.exp2(scores), values[:TOK, cols])
        total = added if total is None else total + added
    return total


def per_head(own, query, blocks, caps, use, groups=KVH):
    if groups == KVH:
        for head in range(QH):
            use(head, head_sums(own, query, blocks, caps, head))
        return

    def some_groups(step, carry):
        for at in range(groups * PER):
            head = step * groups * PER + at
            group = step * groups + at // PER
            use(head, head_sums(own, query, blocks, caps, head, group))
        return carry

    lax.fori_loop(0, KVH // groups, some_groups, 0)


def stored_caps(own, blocks, store):
    readers = []
    for at, block in enumerate(blocks):
        for half, cap in enumerate(cap_of(own, block)):
            store[at, aligned(half, 8)] = jnp.broadcast_to(cap, (8, TOK))
        readers.append(lambda at=at: [store[at, 8 * half : 8 * half + 1] for half in range(2)])
    return readers


def pack_kernel(segments, keys, values, block, tagged):
    rows = lax.broadcasted_iota(jnp.int32, (TAG, WIDE), 0)
    docs = jnp.where(rows < TAG // 2, segments[0], segments[SUB])
    docs = docs.astype(jnp.float32).astype(jnp.bfloat16)
    block[:TOK] = keys[...]
    for target, start in ((block, TOK), (tagged, 0)):
        target[start : start + TOK] = values[...]
        target[start + TOK :] = docs


def own_kernel(query, block, state):
    own = pair_of(block)

    def put(head, sums):
        state[:TOK, aligned(head, 2 * HD)] = sums

    caps = own_cap(own)
    per_head(own, query, [own], [lambda: caps], put)


def pair_of(block):
    return (block.at[:TOK], block.at[TOK:])


def paired(refs, whole):
    refs = iter(refs)
    return [pair_of(next(refs)) if one else (next(refs), next(refs)) for one in whole]


def flat(blocks):
    arrays = [part for block in blocks for part in (block if isinstance(block, tuple) else [block])]
    return arrays, tuple(not isinstance(block, tuple) for block in blocks)


def earlier(steps):
    place = lax.axis_index("ctx")
    y, z = place // 2, place % 2
    return [((y + dy) % 4 * 2 + (z + dz) % 2 < place).astype(jnp.int32) for dy, dz in steps]


def more_kernel(steps, cases, whole, query, *refs):
    count = len(steps)
    own, *blocks = paired(refs[:-3], whole)
    state_in, state, store = refs[-3:]
    flags = earlier(steps)
    code = sum(flag << at for at, flag in enumerate(flags))

    def add(head, sums):
        span = aligned(head, 2 * HD)
        state[:TOK, span] = state_in[:TOK, span] + sums

    rest = jnp.int32(1)
    for chosen, groups in cases:
        fits = (code == sum(1 << at for at in chosen)).astype(jnp.int32)
        rest = rest - fits

        @pl.when(fits > 0)
        def _():
            some = [blocks[at] for at in chosen]
            per_head(own, query, some, stored_caps(own, some, store), add, groups)

    @pl.when(rest > 0)
    def _():
        state[:TOK] = state_in[:TOK]


def last_kernel(steps, whole, query, *refs):
    own, *blocks = paired(refs[:-6], whole)
    state, out, merged, worst, store, sem = refs[-6:]
    flags = earlier(steps)
    pieces = [(start * HD, (end - start) * HD) for start, end in PIECES]

    def out_copy(at):
        span = pl.ds(*pieces[at])
        return pltpu.make_async_copy(merged.at[:, span], out.at[:, span], sem.at[at])

    def put(head, sums):
        merged[:, aligned(head, HD)] = (sums[:, :HD] / sums[:, HD:]).astype(jnp.bfloat16)

    tops = []

    def finish(head, sums):
        sums = sums + state[:TOK, aligned(head, 2 * HD)]
        put(head, sums)
        tops.append(jnp.sum(sums[:, HD:].reshape(TOK // 8, 8, HD), axis=0))
        for at, (start, size) in enumerate(pieces):
            if start + size == (head + 1) * HD:
                out_copy(at).start()
        if head == QH - 1:
            worst[...] = jnp.where(sum(tops) < SAFE, 0.0, 1.0)
            tops.clear()

    @pl.when(flags[0] > 0)
    def _():
        per_head(own, query, blocks[:1], stored_caps(own, blocks[:1], store), finish)

    @pl.when(flags[0] == 0)
    def _():
        for head in range(QH):
            finish(head, 0.0)

    bad = jnp.max(worst[...]) > 0.0
    for at in range(len(pieces)):
        out_copy(at).wait()

    @pl.when(bad)
    def _():
        def one_head(head, carry):
            cols = aligned(head // PER, HD)
            rows = query[:, aligned(head, HD)]

            def allowed(block, at):
                scores = scores_of(rows, block[0][:, cols]) * SCALE
                if at is None:
                    return capped(scores, own_cap(own))
                return jnp.where(flags[at] > 0, capped(scores, cap_of(own, block)), SHUT)

            places = [(own, None)] + [(block, at) for at, block in enumerate(blocks)]
            top = None
            for block, at in places:
                high = jnp.max(allowed(block, at), axis=1, keepdims=True)
                top = high if top is None else jnp.maximum(top, high)
            total = jnp.zeros((TOK, 2 * HD), jnp.float32)
            for block, at in places:
                weights = jnp.exp2(allowed(block, at) - top)
                total = total + weighted(weights, block[1][:TOK, cols])
            put(head, total)
            return carry

        lax.fori_loop(0, QH, one_head, 0)
        for at in range(len(pieces)):
            out_copy(at).start()
        for at in range(len(pieces)):
            out_copy(at).wait()


def params():
    return pltpu.CompilerParams(vmem_limit_bytes=8 * 2**20)


def cost(units):
    work = int(units * QH * TOK * TOK)
    return pl.CostEstimate(flops=work * HD * 4, bytes_accessed=2**20, transcendentals=work)


STATE = jax.ShapeDtypeStruct((TOK, 2 * QH * HD), jnp.float32)
START = jax.ShapeDtypeStruct((START_ROWS, 2 * QH * HD), jnp.float32)


def pack(segments, keys, values):
    return pl.pallas_call(
        pack_kernel,
        in_specs=[SMEM, VMEM, VMEM],
        out_specs=(VMEM, VMEM),
        out_shape=(
            jax.ShapeDtypeStruct((2 * TOK + TAG, WIDE), jnp.bfloat16),
            jax.ShapeDtypeStruct((TOK + TAG, WIDE), jnp.bfloat16),
        ),
        name="pack",
    )(segments, keys, values)


def attend_own(query, own):
    return pl.pallas_call(
        own_kernel,
        in_specs=[VMEM] * 2,
        out_specs=VMEM,
        out_shape=START,
        compiler_params=params(),
        cost_estimate=cost(1),
        name="own",
    )(query, own)


def cap_store(count):
    return pltpu.VMEM((count, 16, TOK), jnp.float32)


def attend_more(name, steps, cases, query, own, blocks, state):
    arrays, whole = flat([own] + blocks)
    return pl.pallas_call(
        functools.partial(more_kernel, steps, cases, whole),
        in_specs=[VMEM] * (2 + len(arrays)),
        out_specs=VMEM,
        out_shape=STATE,
        scratch_shapes=[cap_store(len(steps))],
        compiler_params=params(),
        cost_estimate=cost(len(steps)),
        name=name,
    )(query, *arrays, state)


def attend_last(steps, query, own, blocks, state):
    arrays, whole = flat([own] + blocks)
    return pl.pallas_call(
        functools.partial(last_kernel, steps, whole),
        in_specs=[VMEM] * (2 + len(arrays)),
        out_specs=pl.BlockSpec(memory_space=pl.ANY),
        out_shape=jax.ShapeDtypeStruct((TOK, QH * HD), jnp.bfloat16),
        scratch_shapes=[
            pltpu.VMEM((TOK, QH * HD), jnp.bfloat16),
            pltpu.VMEM((8, HD), jnp.float32),
            cap_store(1),
            pltpu.SemaphoreType.DMA((len(PIECES),)),
        ],
        compiler_params=params(),
        cost_estimate=cost(1),
        name="last",
    )(query, *arrays, state)


def move(value, step_y, step_z, rows=range(4)):
    pairs = []
    for y in rows:
        for z in range(2):
            pairs.append((y * 2 + z, (y + step_y) % 4 * 2 + (z + step_z) % 2))
    return lax.ppermute(value, "ctx", pairs)


def local(query, keys, values, segments):
    up = functools.partial(move, step_y=1, step_z=0)
    down = functools.partial(move, step_y=-1, step_z=0)
    over = functools.partial(move, step_y=0, step_z=1)

    k_down, k_over = down(keys), over(keys)
    own, tagged = pack(segments, keys, values)
    v_down, v_over = down(tagged), over(tagged)
    b_up = up(own)
    state = attend_own(query, own)
    v_down, v_over, state = lax.optimization_barrier((v_down, v_over, state))
    b_down = jnp.concatenate([k_down, v_down], axis=0)
    b_over = jnp.concatenate([k_over, v_over], axis=0)
    b_far, b_down_over, b_up_over = down(b_down), over(b_down), up(b_over, rows=range(3))
    near = [b_up, (k_down, v_down), (k_over, v_over)]
    near_steps = [(-1, 0), (1, 0), (0, 1)]
    state = attend_more("near", near_steps, NEAR_CASES, query, own, near, state)
    b_far, b_down_over, state = lax.optimization_barrier((b_far, b_down_over, state))
    end = [(over(b_far[:TOK]), down(b_down_over[TOK:]))]
    end_steps = [(2, 1)]
    mid = [b_far, b_up_over, b_down_over]
    mid_steps = [(2, 0), (-1, 1), (1, 1)]
    state = attend_more("mid", mid_steps, MID_CASES, query, own, mid, state)
    return attend_last(end_steps + near_steps + mid_steps, query, own, end + near + mid, state)


def solution(mesh):
    placed = (
        P(("dp", "ctx"), None),
        P(("dp", "ctx"), None),
        P(("dp", "ctx"), None),
        P(("dp", "ctx")),
    )
    return jax.shard_map(
        local, mesh=mesh, in_specs=placed, out_specs=P(("dp", "ctx"), None), check_vma=False
    )
```
